32 devices in a mesh: blk: 8 (over z, y), shard: 4 (over x, core).
Axes of the slice: x: 2, y: 2, z: 4, core: 2. Of those that a mesh axis runs over, the one named last changes fastest.
Arguments:
- weights: bfloat16 [8, 2, 5120, 5120], P('blk', None, 'shard'), may hold values from -35 to 35
- q_warm: bfloat16 [8, 2, 8, 5120], P('blk'), may hold values from -6 to 6
Outputs:
- new_weights: bfloat16 [8, 2, 5120, 5120], P('blk', None, 'shard')
- q_next: bfloat16 [8, 2, 8, 5120], P('blk')
The draws below stay inside these ranges and needn't reach their ends.
All inputs are finite; a program needn't handle non-finite values.
Results may differ from the reference program's by a relative error of at most 0.0046.
Values may be sent and summed in bfloat16 or wider, within the bound.
A program may use at most 256 MiB of HBM per device.

```python
import jax
import jax.numpy as jnp
from jax import lax

D = 5120
MATS = 2
RANK = 8
REPLICAS = 8


def draw_weights(key, part):
    key = jax.random.fold_in(key, 11)
    base_key, row_key, col_key = jax.random.split(key, 3)
    full_shape = (REPLICAS, MATS, D, D)
    position = jnp.arange(D, dtype=jnp.float32) / (D - 1)
    row_scale = jnp.exp(jnp.log(3.0) * (position - 0.5))[None, :, None]
    row_scale = row_scale * jnp.exp(jax.random.uniform(row_key, (MATS, D, 1), minval=-0.7, maxval=0.7))
    col_scale = jnp.exp(jax.random.uniform(col_key, (MATS, 1, D), minval=-0.7, maxval=0.7))
    values = jax.random.truncated_normal(base_key, -5.0, 5.0, full_shape)
    return (values * row_scale[None] * col_scale[None]).astype(jnp.bfloat16)


def levels(key, dims, cuts, smallest, top_value):
    def one(dim, parts):
        draws = jax.random.uniform(jax.random.fold_in(jax.random.fold_in(key, 6), dim), (parts,), jnp.float32, smallest / len(cuts), top_value / len(cuts))
        return jnp.repeat(jnp.exp(draws), dims[dim] // parts).reshape((-1,) + (1,) * (len(dims) - dim - 1))

    level = one(*cuts[0])
    for cut in cuts[1:]:
        level = level * one(*cut)
    return level


def gaussian(stream_key, shape, scale, most, pieces=(), held_as=jnp.bfloat16):
    drawn = jax.random.normal(stream_key, shape, jnp.float32) * scale
    if len(pieces) > 0:
        drawn = levels(stream_key, shape, pieces, -0.22, 0.18) * drawn
    return jnp.clip(drawn, min=-most, max=most).astype(held_as)


def setup_inputs(seed: int = 0) -> dict:
    keys = jax.random.split(jax.random.key(seed), 3)
    return {
        "weights": draw_weights(jax.random.fold_in(keys[2], 71), 0),
        "q_warm": gaussian(keys[1], (REPLICAS, MATS, RANK, D), 1.0, 6.0, ((0, 8),)),
    }


def substitute(factor, lower_tri):
    result_rows = []
    for position in range(factor.shape[-2]):
        current = factor[..., position, :]
        for earlier in range(position):
            current = current - lower_tri[..., position, earlier][..., None] * result_rows[earlier]
        result_rows.append(current / lower_tri[..., position, position][..., None])
    return jnp.stack(result_rows, axis=-2)

def orthonormal(factor):
    gram = jnp.einsum('...kr,...jr->...kj', factor, factor, precision=lax.Precision.HIGHEST)
    lower_tri = jnp.linalg.cholesky(gram)
    return substitute(factor, lower_tri)

def reference(weights, q_warm):
    q_left = jnp.roll(q_warm, 1, axis=0)

    def project(inputs):
        matrix, right_start, left_start = inputs
        wide = matrix.astype(jnp.float32)
        first = jnp.einsum('mkc,mrc->mkr', right_start.astype(jnp.float32), wide, precision=lax.Precision.HIGHEST)
        second = jnp.einsum('mkc,mrc->mkr', left_start.astype(jnp.float32), wide, precision=lax.Precision.HIGHEST)
        return (first, second)
    a_right, a_left = lax.map(project, (weights, q_warm, q_left))
    p_right = a_right - jnp.roll(a_left, -1, axis=0)
    h_right = orthonormal(p_right)
    h_left = jnp.roll(h_right, 1, axis=0)
    hb_right = lax.optimization_barrier(h_right.astype(jnp.bfloat16))
    hb_left = jnp.roll(hb_right, 1, axis=0)

    def spread(inputs):
        matrix, right_rows, left_rows = inputs
        wide = matrix.astype(jnp.float32)
        first = jnp.einsum('mkr,mrc->mkc', right_rows.astype(jnp.float32), wide, precision=lax.Precision.HIGHEST)
        second = jnp.einsum('mkr,mrc->mkc', left_rows.astype(jnp.float32), wide, precision=lax.Precision.HIGHEST)
        return (first, second)
    s_right, s_left = lax.map(spread, (weights, hb_right, hb_left))
    c_right = s_right - jnp.roll(s_left, -1, axis=0)
    c_left = jnp.roll(c_right, 1, axis=0)

    def update(inputs):
        matrix, right_rows, left_rows, right_cols, left_cols = inputs
        correction = jnp.einsum('mkr,mkc->mrc', left_rows, left_cols, precision=lax.Precision.HIGHEST)
        correction = correction - jnp.einsum('mkr,mkc->mrc', right_rows, right_cols, precision=lax.Precision.HIGHEST)
        return (matrix.astype(jnp.float32) + 0.5 * correction).astype(jnp.bfloat16)
    new_weights = lax.map(update, (weights, h_right, h_left, c_right, c_left))
    return (new_weights, c_right.astype(jnp.bfloat16))
```

```python
import functools

import jax
import jax.numpy as jnp
from jax import lax
from jax.experimental import pallas as pl
from jax.experimental.pallas import tpu as pltpu
from jax.sharding import PartitionSpec as P

F32 = jnp.float32
BF16 = jnp.bfloat16
NT = (((1,), (1,)), ((), ()))
NN = (((1,), (0,)), ((), ()))
TN = (((0,), (0,)), ((), ()))


def factors_kernel(
    nb, ns, mats, rank, rows, width, chunk,
    q_ref, w_ref,
    h_ref, c_ref,
    w_v, q_in, qq, a_v, ar_in, al_in, p_v, g_out, g_in, hb,
    x_out, x_in, y_out, z_in, t_v, tr_in, tl_in, c_all,
    w_sem, q_sem, a_sem, g_ssem, g_rsem, x_sem, z_sem, t_sem, c_ssem, c_rsem,
):
    b, s = lax.axis_index("blk"), lax.axis_index("shard")
    nxt, prv = lax.rem(b + 1, nb), lax.rem(b + nb - 1, nb)
    core = lax.rem(s, 2)
    mine = s // 2
    other = mine * 2 + (1 - core)
    nr = ns // 2
    part = width // ns
    pieces = rows // chunk

    loads = []
    for m in range(mats):
        for t in range(pieces):
            where = pl.ds(t * chunk, chunk)
            load = pltpu.make_async_copy(
                w_ref.at[0, m, where, :], w_v.at[m, where, :], w_sem.at[m, t]
            )
            load.start()
            loads.append(load)

    barrier = pltpu.get_barrier_semaphore()
    partners = [(nxt, s), (prv, s)]
    partners += [(b, lax.rem(s + d, ns)) for d in range(1, ns)]
    for partner in partners:
        pl.semaphore_signal(
            barrier, inc=1, device_id=partner, device_id_type=pl.DeviceIdType.MESH
        )
    pl.semaphore_wait(barrier, len(partners))

    sent = []

    def send(src, dst, ssem, rsem, device):
        copy = pltpu.make_async_remote_copy(
            src_ref=src, dst_ref=dst, send_sem=ssem, recv_sem=rsem,
            device_id=device, device_id_type=pl.DeviceIdType.MESH,
        )
        copy.start()
        sent.append(copy)
        return copy

    q_copy = send(q_ref, q_in, q_sem.at[0], q_sem.at[1], (nxt, s))
    q_copy.wait_recv()
    own_q = q_ref[...].astype(F32)
    far_q = q_in[...].astype(F32)
    for m in range(mats):
        low, high = m * rank, (m + 1) * rank
        qq[m] = jnp.concatenate([own_q[low:high], far_q[low:high]], axis=0).astype(BF16)

    a_copies = []
    for m in range(mats):
        for t in range(pieces):
            loads[m * pieces + t].wait()
            a_v[m, :, t * chunk:(t + 1) * chunk] = lax.dot_general(
                qq[m], w_v[m, t * chunk:(t + 1) * chunk, :], NT, preferred_element_type=F32
            )
        a_copies.append((
            send(a_v.at[m, 0:rank], ar_in.at[m], a_sem.at[0, m], a_sem.at[1, m], (nxt, s)),
            send(a_v.at[m, rank:2 * rank], al_in.at[m], a_sem.at[2, m], a_sem.at[3, m], (prv, s)),
        ))

    g_copies = []
    for m in range(mats):
        for copy in a_copies[m]:
            copy.wait_recv()
        p = jnp.concatenate(
            [a_v[m, 0:rank] - al_in[m], ar_in[m] - a_v[m, rank:2 * rank]], axis=0
        )
        p_v[m] = p
        g_out[m, :, 0:2 * rank] = lax.dot_general(
            p, p, NT, precision=lax.Precision.HIGHEST, preferred_element_type=F32
        )
        g_copies.append([
            send(
                g_out.at[m], g_in.at[m, d - 1], g_ssem.at[m, d - 1], g_rsem.at[m, d - 1],
                (b, lax.rem(s + d, ns)),
            )
            for d in range(1, ns)
        ])

    def orthonormalize(m):
        for copy in g_copies[m]:
            copy.wait_recv()
        gram = g_out[m]
        for d in range(1, ns):
            gram = gram + g_in[m, d - 1]
        for e in range(2):
            low = e * rank
            left = gram[low:low + rank, low:low + rank]
            right = p_v[m, low:low + rank]
            place = lax.broadcasted_iota(jnp.int32, (rank, 1), 0)
            diagonal = jnp.ones((rank, 1), F32)
            for k in range(rank):
                pivot = left[k:k + 1, k:k + 1]
                diagonal = jnp.where(place == k, pivot, diagonal)
                if k < rank - 1:
                    factor = jnp.where(place > k, left[:, k:k + 1] / pivot, 0.0)
                    left = left - factor * left[k:k + 1]
                    right = right - factor * right[k:k + 1]
            right = right * (1.0 / jnp.sqrt(diagonal))
            p_v[m, low:low + rank] = right
        h = p_v[m]
        hb[m] = h.astype(BF16)
        row = lax.broadcasted_iota(jnp.int32, (2 * rank, 1), 0)
        scaled = h * jnp.where(row < rank, -0.5, 0.5)
        wide = scaled.astype(BF16)
        h_ref[m] = jnp.concatenate([wide, (scaled - wide.astype(F32)).astype(BF16)], axis=0)

    def product(m, owner):
        where = pl.ds(pl.multiple_of(owner * part, 128), part)
        return lax.dot_general(hb[m], w_v[m, :, where], NN, preferred_element_type=F32)

    x_copies, z_copies, t_copies, c_copies = {}, {}, {}, {}

    def for_other_core(m):
        for d in list(range(1, nr)) + [0]:
            group = lax.rem(mine + d, nr)
            x_out[m, d] = product(m, group * 2 + (1 - core))
            x_copies[m, d] = send(
                x_out.at[m, d], x_in.at[m, d], x_sem.at[0, m, d], x_sem.at[1, m, d], (b, other)
            )

    def for_this_core(m):
        for d in range(1, nr):
            group = lax.rem(mine + d, nr)
            own = product(m, group * 2 + core)
            x_copies[m, d].wait_recv()
            y_out[m, d - 1] = own + x_in[m, d]
            z_copies[m, d] = send(
                y_out.at[m, d - 1], z_in.at[m, d - 1],
                z_sem.at[0, m, d - 1], z_sem.at[1, m, d - 1], (b, group * 2 + core),
            )
        own = product(m, s)
        x_copies[m, 0].wait_recv()
        t_v[m] = own + x_in[m, 0]

    def to_neighbours(m):
        total = t_v[m]
        for d in range(1, nr):
            z_copies[m, d].wait_recv()
            total = total + z_in[m, d - 1]
        t_v[m] = total
        t_copies[m] = (
            send(t_v.at[m, 0:rank], tr_in.at[m], t_sem.at[0, m], t_sem.at[1, m], (nxt, s)),
            send(t_v.at[m, rank:2 * rank], tl_in.at[m], t_sem.at[2, m], t_sem.at[3, m], (prv, s)),
        )

    def spread_columns(m):
        for copy in t_copies[m]:
            copy.wait_recv()
        c_all[m, s] = jnp.concatenate(
            [t_v[m, 0:rank] - tl_in[m], tr_in[m] - t_v[m, rank:2 * rank]], axis=0
        ).astype(BF16)
        c_copies[m] = [
            send(
                c_all.at[m, s], c_all.at[m, s], c_ssem.at[m, d - 1], c_rsem.at[m, d - 1],
                (b, lax.rem(s + d, ns)),
            )
            for d in range(1, ns)
        ]

    orthonormalize(0)
    for_other_core(0)
    for_this_core(0)
    for m in range(1, mats):
        orthonormalize(m)
        for_other_core(m)
        to_neighbours(m - 1)
        for_this_core(m)
        spread_columns(m - 1)
    to_neighbours(mats - 1)
    spread_columns(mats - 1)

    for m in range(mats):
        for copy in c_copies[m]:
            copy.wait_recv()
        for owner in range(ns):
            c_ref[m, :, owner * part:(owner + 1) * part] = c_all[m, owner]
    for copy in sent:
        copy.wait_send()


def update_kernel(rank, step, w_ref, h_ref, c_ref, out_ref, q_ref):
    width = w_ref.shape[-1]
    for start in range(0, width, step):
        where = slice(start, start + step)
        cols = c_ref[0, :, where]
        both = jnp.concatenate([cols, cols], axis=0)
        change = lax.dot_general(h_ref[0], both, TN, preferred_element_type=F32)
        out_ref[0, 0, :, where] = (w_ref[0, 0, :, where].astype(F32) + change).astype(BF16)

    @pl.when(pl.program_id(1) == 0)
    def _():
        q_ref[0, 0] = c_ref[0].astype(F32)[0:rank].astype(BF16)


def per_device(nb, ns, weights, q_warm):
    _, mats, rows, width = weights.shape
    rank = q_warm.shape[2]
    chunk = 256 if rows % 256 == 0 else 128
    nr, part = ns // 2, width // ns
    vmem, dma = pltpu.VMEM, pltpu.SemaphoreType.DMA
    whole = pl.BlockSpec(memory_space=pltpu.VMEM)
    flops = 2 * 2 * mats * 2 * rank * rows * width
    h, c = pl.pallas_call(
        functools.partial(factors_kernel, nb, ns, mats, rank, rows, width, chunk),
        out_shape=(
            jax.ShapeDtypeStruct((mats, 4 * rank, rows), BF16),
            jax.ShapeDtypeStruct((mats, 2 * rank, width), BF16),
        ),
        in_specs=[whole, pl.BlockSpec(memory_space=pl.ANY)],
        out_specs=(whole, whole),
        scratch_shapes=[
            vmem((mats, rows, width), BF16),
            vmem((mats * rank, width), BF16),
            vmem((mats, 2 * rank, width), BF16),
            vmem((mats, 2 * rank, rows), F32),
            vmem((mats, rank, rows), F32),
            vmem((mats, rank, rows), F32),
            vmem((mats, 2 * rank, rows), F32),
            vmem((mats, 2 * rank, 128), F32),
            vmem((mats, ns - 1, 2 * rank, 128), F32),
            vmem((mats, 2 * rank, rows), BF16),
            vmem((mats, nr, 2 * rank, part), F32),
            vmem((mats, nr, 2 * rank, part), F32),
            vmem((mats, nr - 1, 2 * rank, part), F32),
            vmem((mats, nr - 1, 2 * rank, part), F32),
            vmem((mats, 2 * rank, part), F32),
            vmem((mats, rank, part), F32),
            vmem((mats, rank, part), F32),
            vmem((mats, ns, 2 * rank, part), BF16),
            dma((mats, rows // chunk)),
            dma((2,)),
            dma((4, mats)),
            dma((mats, ns - 1)),
            dma((mats, ns - 1)),
            dma((2, mats, nr)),
            dma((2, mats, nr - 1)),
            dma((4, mats)),
            dma((mats, ns - 1)),
            dma((mats, ns - 1)),
        ],
        compiler_params=pltpu.CompilerParams(
            collective_id=0, has_side_effects=True, vmem_limit_bytes=50 * 2**20
        ),
        cost_estimate=pl.CostEstimate(
            flops=flops, bytes_accessed=weights.size * 2, transcendentals=0
        ),
        name="factors",
    )(q_warm.reshape(mats * rank, width), weights)
    step = 1280 if width % 1280 == 0 else width
    new_weights, q_next = pl.pallas_call(
        functools.partial(update_kernel, rank, step),
        grid=(mats, rows // chunk),
        out_shape=(
            jax.ShapeDtypeStruct(weights.shape, BF16),
            jax.ShapeDtypeStruct(q_warm.shape, BF16),
        ),
        in_specs=[
            pl.BlockSpec((1, 1, chunk, width), lambda m, t: (0, m, t, 0)),
            pl.BlockSpec((1, 4 * rank, chunk), lambda m, t: (m, 0, t)),
            pl.BlockSpec((1, 2 * rank, width), lambda m, t: (m, 0, 0)),
        ],
        out_specs=(
            pl.BlockSpec((1, 1, chunk, width), lambda m, t: (0, m, t, 0)),
            pl.BlockSpec((1, 1, rank, width), lambda m, t: (0, m, 0, 0)),
        ),
        compiler_params=pltpu.CompilerParams(vmem_limit_bytes=50 * 2**20),
        cost_estimate=pl.CostEstimate(
            flops=flops // 2, bytes_accessed=weights.size * 4, transcendentals=0
        ),
        name="update",
    )(weights, h, c)
    return new_weights, q_next


def solution(mesh):
    placed = (P("blk", None, "shard", None), P("blk", None, None, None))
    return jax.shard_map(
        functools.partial(per_device, mesh.shape["blk"], mesh.shape["shard"]),
        mesh=mesh,
        in_specs=placed,
        out_specs=placed,
        check_vma=False,
    )
```

```python
import functools

import jax
import jax.numpy as jnp
from jax import lax
from jax.experimental import pallas as pl
from jax.experimental.pallas import tpu as pltpu
from jax.sharding import PartitionSpec as P

F32 = jnp.float32
BF16 = jnp.bfloat16
NT = (((1,), (1,)), ((), ()))
NN = (((1,), (0,)), ((), ()))
TN = (((0,), (0,)), ((), ()))


def factors_kernel(
    nb, ns, mats, rank, rows, width, chunk,
    q_ref, w_ref,
    h_ref, c_ref, w_v,
    q_own, q_in, qq, a_v, ar_in, al_in, p_v, g_out, g_in, hb,
    s_all, x_out, x_in, y_out, z_in, t_v, tr_in, tl_in, c_all,
    w_sem, q_sem, a_sem, g_ssem, g_rsem, x_sem, z_sem, t_sem, c_ssem, c_rsem,
):
    b, s = lax.axis_index("blk"), lax.axis_index("shard")
    nxt, prv = lax.rem(b + 1, nb), lax.rem(b + nb - 1, nb)
    core = lax.rem(s, 2)
    mine = s // 2
    other = mine * 2 + (1 - core)
    nr = ns // 2
    part = width // ns
    pieces = rows // chunk

    local_q = pltpu.make_async_copy(q_ref, q_own, q_sem.at[4])
    local_q.start()
    loads = []
    for m in range(mats):
        for t in range(pieces):
            where = pl.ds(t * chunk, chunk)
            load = pltpu.make_async_copy(
                w_ref.at[0, m, where, :], w_v.at[m, where, :], w_sem.at[m, t]
            )
            load.start()
            loads.append(load)

    barrier = pltpu.get_barrier_semaphore()
    partners = [(nxt, s), (prv, s)]
    partners += [(b, lax.rem(s + d, ns)) for d in range(1, ns)]
    for partner in partners:
        pl.semaphore_signal(
            barrier, inc=1, device_id=partner, device_id_type=pl.DeviceIdType.MESH
        )
    pl.semaphore_wait(barrier, len(partners))

    sent = []

    def send(src, dst, ssem, rsem, device):
        copy = pltpu.make_async_remote_copy(
            src_ref=src, dst_ref=dst, send_sem=ssem, recv_sem=rsem,
            device_id=device, device_id_type=pl.DeviceIdType.MESH,
        )
        copy.start()
        sent.append(copy)
        return copy

    local_q.wait()
    half = pl.ds(pl.multiple_of(core * (width // 2), 128), width // 2)
    send(
        q_own.at[:, half], q_in.at[:, half], q_sem.at[0], q_sem.at[1], (nxt, s)
    ).wait_recv()
    send(
        q_in.at[:, half], q_in.at[:, half], q_sem.at[2], q_sem.at[3], (b, other)
    ).wait_recv()
    own_q = q_own[...].astype(F32)
    far_q = q_in[...].astype(F32)
    for m in range(mats):
        low, high = m * rank, (m + 1) * rank
        qq[m] = jnp.concatenate([own_q[low:high], far_q[low:high]], axis=0).astype(BF16)

    a_copies = []
    for m in range(mats):
        for t in range(pieces):
            loads[m * pieces + t].wait()
            a_v[m, :, t * chunk:(t + 1) * chunk] = lax.dot_general(
                qq[m], w_v[m, t * chunk:(t + 1) * chunk, :], NT, preferred_element_type=F32
            )
        a_copies.append((
            send(a_v.at[m, 0:rank], ar_in.at[m], a_sem.at[0, m], a_sem.at[1, m], (nxt, s)),
            send(a_v.at[m, rank:2 * rank], al_in.at[m], a_sem.at[2, m], a_sem.at[3, m], (prv, s)),
        ))

    g_copies = {}

    def send_gram(m):
        for copy in a_copies[m]:
            copy.wait_recv()
        p = jnp.concatenate(
            [a_v[m, 0:rank] - al_in[m], ar_in[m] - a_v[m, rank:2 * rank]], axis=0
        )
        p_v[m] = p
        g_out[m, :, 0:2 * rank] = lax.dot_general(
            p, p, NT, precision=lax.Precision.HIGHEST, preferred_element_type=F32
        )
        g_copies[m] = [
            send(
                g_out.at[m], g_in.at[m, d - 1], g_ssem.at[m, d - 1], g_rsem.at[m, d - 1],
                (b, lax.rem(s + d, ns)),
            )
            for d in range(1, ns)
        ]

    def orthonormalize(m):
        for copy in g_copies[m]:
            copy.wait_recv()
        gram = g_out[m]
        for d in range(1, ns):
            gram = gram + g_in[m, d - 1]
        for e in range(2):
            low = e * rank
            left = gram[low:low + rank, low:low + rank]
            right = p_v[m, low:low + rank]
            place = lax.broadcasted_iota(jnp.int32, (rank, 1), 0)
            diagonal = jnp.ones((rank, 1), F32)
            for k in range(rank):
                pivot = left[k:k + 1, k:k + 1]
                diagonal = jnp.where(place == k, pivot, diagonal)
                if k < rank - 1:
                    factor = jnp.where(place > k, left[:, k:k + 1] / pivot, 0.0)
                    left = left - factor * left[k:k + 1]
                    right = right - factor * right[k:k + 1]
            right = right * (1.0 / jnp.sqrt(diagonal))
            p_v[m, low:low + rank] = right
        h = p_v[m]
        hb[m] = h.astype(BF16)
        row = lax.broadcasted_iota(jnp.int32, (2 * rank, 1), 0)
        scaled = h * jnp.where(row < rank, -0.5, 0.5)
        wide = scaled.astype(BF16)
        h_ref[m] = jnp.concatenate([wide, (scaled - wide.astype(F32)).astype(BF16)], axis=0)

    def prepare(m):
        if part % 128:
            for owner in range(ns):
                s_all[m, owner] = lax.dot_general(
                    hb[m], w_v[m, :, owner * part:(owner + 1) * part], NN,
                    preferred_element_type=F32,
                )

    def product(m, owner):
        if part % 128:
            return s_all[m, owner]
        where = pl.ds(pl.multiple_of(owner * part, 128), part)
        return lax.dot_general(hb[m], w_v[m, :, where], NN, preferred_element_type=F32)

    x_copies, z_copies, t_copies, c_copies = {}, {}, {}, {}

    def for_other_core(m):
        prepare(m)
        for d in list(range(1, nr)) + [0]:
            group = lax.rem(mine + d, nr)
            x_out[m, d] = product(m, group * 2 + (1 - core))
            x_copies[m, d] = send(
                x_out.at[m, d], x_in.at[m, d], x_sem.at[0, m, d], x_sem.at[1, m, d], (b, other)
            )

    def for_this_core(m):
        for d in range(1, nr):
            group = lax.rem(mine + d, nr)
            own = product(m, group * 2 + core)
            x_copies[m, d].wait_recv()
            y_out[m, d - 1] = own + x_in[m, d]
            z_copies[m, d] = send(
                y_out.at[m, d - 1], z_in.at[m, d - 1],
                z_sem.at[0, m, d - 1], z_sem.at[1, m, d - 1], (b, group * 2 + core),
            )
        own = product(m, s)
        x_copies[m, 0].wait_recv()
        t_v[m] = own + x_in[m, 0]

    def to_neighbours(m):
        total = t_v[m]
        for d in range(1, nr):
            z_copies[m, d].wait_recv()
            total = total + z_in[m, d - 1]
        t_v[m] = total
        t_copies[m] = (
            send(t_v.at[m, 0:rank], tr_in.at[m], t_sem.at[0, m], t_sem.at[1, m], (nxt, s)),
            send(t_v.at[m, rank:2 * rank], tl_in.at[m], t_sem.at[2, m], t_sem.at[3, m], (prv, s)),
        )

    def spread_columns(m):
        for copy in t_copies[m]:
            copy.wait_recv()
        c_all[m, s] = jnp.concatenate(
            [t_v[m, 0:rank] - tl_in[m], tr_in[m] - t_v[m, rank:2 * rank]], axis=0
        ).astype(BF16)
        c_copies[m] = [
            send(
                c_all.at[m, s], c_all.at[m, s], c_ssem.at[m, d - 1], c_rsem.at[m, d - 1],
                (b, lax.rem(s + d, ns)),
            )
            for d in range(1, ns)
        ]

    send_gram(0)
    orthonormalize(0)
    for_other_core(0)
    for m in range(1, mats):
        send_gram(m)
        for_this_core(m - 1)
        orthonormalize(m)
        for_other_core(m)
        to_neighbours(m - 1)
    for_this_core(mats - 1)
    to_neighbours(mats - 1)
    for m in range(mats):
        spread_columns(m)

    for m in range(mats):
        for copy in c_copies[m]:
            copy.wait_recv()
        for owner in range(ns):
            c_ref[m, :, owner * part:(owner + 1) * part] = c_all[m, owner]
    for copy in sent:
        copy.wait_send()


def update_kernel(rank, chunk, step, w_ref, h_ref, c_ref, out_ref, q_ref, slots, out_sem, q_v, q_sem):
    mats, rows, width = w_ref.shape
    count = slots.shape[0]
    q_copies, copies = [], []
    for m in range(mats):
        cols = c_ref[m]
        q_v[m] = cols.astype(F32)[0:rank].astype(BF16)
        copy = pltpu.make_async_copy(q_v.at[m], q_ref.at[0, m], q_sem.at[m])
        copy.start()
        q_copies.append(copy)
        both = jnp.concatenate([cols, cols], axis=0)
        for first in range(0, rows, chunk):
            here = slice(first, first + chunk)
            slot = len(copies) % count
            if len(copies) >= count:
                copies[-count].wait()
            for start in range(0, width, step):
                where = slice(start, start + step)
                change = lax.dot_general(
                    h_ref[m, :, here], both[:, where], TN, preferred_element_type=F32
                )
                slots[slot, :, where] = (w_ref[m, here, where].astype(F32) + change).astype(BF16)
            copy = pltpu.make_async_copy(
                slots.at[slot], out_ref.at[0, m, pl.ds(first, chunk), :], out_sem.at[slot]
            )
            copy.start()
            copies.append(copy)
    for copy in copies[-count:] + q_copies:
        copy.wait()


def per_device(nb, ns, weights, q_warm):
    _, mats, rows, width = weights.shape
    rank = q_warm.shape[2]
    chunk = next(size for size in (256, 128, rows) if rows % size == 0)
    tile = next(size for size in (128, 64, 16) if rows % size == 0)
    nr, part = ns // 2, width // ns
    vmem, dma = pltpu.VMEM, pltpu.SemaphoreType.DMA
    whole = pl.BlockSpec(memory_space=pltpu.VMEM)
    hbm = pl.BlockSpec(memory_space=pltpu.HBM)
    flops = 2 * 2 * mats * 2 * rank * rows * width
    h, c, held = pl.pallas_call(
        functools.partial(factors_kernel, nb, ns, mats, rank, rows, width, chunk),
        out_shape=(
            jax.ShapeDtypeStruct((mats, 4 * rank, rows), BF16),
            jax.ShapeDtypeStruct((mats, 2 * rank, width), BF16),
            jax.ShapeDtypeStruct((mats, rows, width), BF16),
        ),
        in_specs=[hbm, hbm],
        out_specs=(whole, whole, whole),
        scratch_shapes=[
            vmem((mats * rank, width), BF16),
            vmem((mats * rank, width), BF16),
            vmem((mats, 2 * rank, width), BF16),
            vmem((mats, 2 * rank, rows), F32),
            vmem((mats, rank, rows), F32),
            vmem((mats, rank, rows), F32),
            vmem((mats, 2 * rank, rows), F32),
            vmem((mats, 2 * rank, 128), F32),
            vmem((mats, ns - 1, 2 * rank, 128), F32),
            vmem((mats, 2 * rank, rows), BF16),
            vmem((mats, ns if part % 128 else 1, 2 * rank, part), F32),
            vmem((mats, nr, 2 * rank, part), F32),
            vmem((mats, nr, 2 * rank, part), F32),
            vmem((mats, nr - 1, 2 * rank, part), F32),
            vmem((mats, nr - 1, 2 * rank, part), F32),
            vmem((mats, 2 * rank, part), F32),
            vmem((mats, rank, part), F32),
            vmem((mats, rank, part), F32),
            vmem((mats, ns, 2 * rank, part), BF16),
            dma((mats, rows // chunk)),
            dma((5,)),
            dma((4, mats)),
            dma((mats, ns - 1)),
            dma((mats, ns - 1)),
            dma((2, mats, nr)),
            dma((2, mats, nr - 1)),
            dma((4, mats)),
            dma((mats, ns - 1)),
            dma((mats, ns - 1)),
        ],
        compiler_params=pltpu.CompilerParams(
            collective_id=0, has_side_effects=True, vmem_limit_bytes=16 * 2**20
        ),
        cost_estimate=pl.CostEstimate(
            flops=flops, bytes_accessed=weights.size * 2, transcendentals=0
        ),
        name="factors",
    )(q_warm.reshape(mats * rank, width), weights)
    step = 512 if width % 512 == 0 else width
    new_weights, q_next = pl.pallas_call(
        functools.partial(update_kernel, rank, tile, step),
        out_shape=(
            jax.ShapeDtypeStruct(weights.shape, BF16),
            jax.ShapeDtypeStruct(q_warm.shape, BF16),
        ),
        in_specs=[whole, whole, whole],
        out_specs=(hbm, hbm),
        scratch_shapes=[
            vmem((3, tile, width), BF16),
            dma((3,)),
            vmem((mats, rank, width), BF16),
            dma((mats,)),
        ],
        compiler_params=pltpu.CompilerParams(vmem_limit_bytes=16 * 2**20),
        cost_estimate=pl.CostEstimate(
            flops=flops // 2, bytes_accessed=weights.size * 2, transcendentals=0
        ),
        name="update",
    )(held, h, c)
    return new_weights, q_next


def solution(mesh):
    placed = (P("blk", None, "shard", None), P("blk", None, None, None))
    return jax.shard_map(
        functools.partial(per_device, mesh.shape["blk"], mesh.shape["shard"]),
        mesh=mesh,
        in_specs=placed,
        out_specs=placed,
        check_vma=False,
    )
```
